256 devices in a mesh: section: 8 (over x, z_hi), expert: 32 (over y, z_lo, core).
Axes of the slice: x: 4, y: 4, z: 8 (z_hi: 2, z_lo: 4; z = z_hi * 4 + z_lo), core: 2. Of those that a mesh axis runs over, the one named last changes fastest.
Arguments:
- forward_start: bfloat16 [8, 1536, 3584], P('section', 'expert'), may hold values from -6 to 6
- forward_feed: bfloat16 [1, 1536, 3584], P(None, 'expert'), may hold values from -6 to 6
- backward_start: bfloat16 [8, 1536, 3584], P('section', 'expert'), may hold values from -6 to 6
- backward_feed: bfloat16 [1, 1536, 3584], P(None, 'expert'), may hold values from -6 to 6
- saved_inputs: bfloat16 [8, 2, 1536, 3584], P('section', None, 'expert'), may hold values from -6 to 6
- expert_picks: int32 [8, 2, 2, 1536, 1], P('section', None, None, 'expert'), may hold values from 0 to 7; in each aligned block of 48 rows (0 to 47, 48 to 95, ..., all dimensions but the last counted through in order) at most 8 rows name the same one
- pick_weights: float32 [8, 2, 2, 1536, 1], P('section', None, None, 'expert'), may hold values from 0.5 to 2.5
- norm_gain: bfloat16 [8, 3584], P('section'), may hold values from 0.19921875 to 1.796875
- w_gate: bfloat16 [8, 3584, 8192], P('section', None, 'expert'), may hold values from -0.09375 to 0.09375
- w_up: bfloat16 [8, 3584, 8192], P('section', None, 'expert'), may hold values from -0.09375 to 0.09375
- w_down: bfloat16 [8, 8192, 3584], P('section', 'expert'), may hold values from -0.1875 to 0.1875
Outputs:
- section_outputs: bfloat16 [8, 2, 1536, 3584], P('section', None, 'expert')
- input_grads: bfloat16 [8, 2, 1536, 3584], P('section', None, 'expert')
The draws below stay inside these ranges and needn't reach their ends.
Inputs may be any that keep to these rules, and one draw needn't show every extreme that they name: `expert_picks`: in the rows of one device (aligned blocks of 48 tokens of a section, tick and pass) no expert is picked by more than 8 rows, and some expert is picked by exactly 8; the 1 picks of a row differ.
All inputs are finite; a program needn't handle non-finite values.
Results may differ from the reference program's by a relative error of at most 0.011.
Values may be sent and summed in bfloat16 or wider, within the bound.
No kernel may reach another device: no remote copies, remote signals or barrier semaphores. Data moves between devices by JAX's collectives and lax.ppermute only.
A program may use at most 128 MiB of HBM per device.

```python
import math
import jax
import jax.numpy as jnp
import numpy as np
from jax import lax

D = 3584
FF = 1024
GROUP = 4
TOP = 1
TOK_DEV = 48
TICKS = 2
FF_SH = 256
EXPERTS = 8
CAP = 8
TOKENS = 1536
SECTIONS = 8
N_EXPERT = 32


def levels(rng, extent, pieces, smallest, high):
    loudness = 1.0
    for dim, shards_of in pieces:
        heights = jax.random.uniform(jax.random.fold_in(jax.random.fold_in(rng, 6), dim), (shards_of,), jnp.float32, smallest / len(pieces), high / len(pieces))
        loudness = loudness * jnp.repeat(jnp.exp(heights), extent[dim] // shards_of).reshape((-1,) + (1,) * (len(extent) - 1 - dim))
    return loudness


def shared_out(rng, own, number, rows, amount, top, limit, lean):
    ranking = jax.random.permutation(rng, amount)
    crowded, ordinary = load_shares(amount, rows * top, limit, lean, True), load_shares(amount, rows * top, limit, lean, False)
    places = jnp.arange(amount)

    def named(lengths, offset_by):
        used = int((lengths > 0).sum())
        fixed = max(1, used // 4)
        moved = fixed + (places - fixed + offset_by * (used - fixed)) % max(1, amount - fixed)
        return jnp.zeros((amount,), jnp.int32).at[ranking[jnp.where(places < fixed, places, moved)]].set(jnp.asarray(lengths, jnp.int32))

    lengths = jnp.where(number % 4 == 0, named(crowded, number // 4), named(ordinary, number - number // 4 - 1))
    mixed = jax.random.permutation(jax.random.fold_in(own, 3), amount)
    giver, sink = mixed[0:amount // 2 * 2:2], mixed[1:amount // 2 * 2:2]
    margin = jnp.minimum(lengths[giver] - 1, limit - lengths[sink]) // 2
    margin = jnp.where((giver == ranking[0]) | (sink == ranking[0]) | (lengths[sink] == 0), 0, jnp.maximum(margin, 0))
    moved = jax.random.randint(jax.random.fold_in(own, 4), (amount // 2,), 0, 1 << 20) % (margin + 1)
    lengths = lengths.at[giver].add(-moved).at[sink].add(moved)
    items = jnp.searchsorted(jnp.cumsum(lengths), jnp.arange(rows * top), side="right").astype(jnp.int32)
    table = items.reshape(top, rows).T
    table = table[jax.random.permutation(jax.random.fold_in(own, 1), rows)]
    offset_by = jax.random.randint(jax.random.fold_in(own, 2), (rows, 1), 0, top)
    return jnp.take_along_axis(table, (jnp.arange(top)[None, :] + offset_by) % top, axis=1)


def load_shares(number_of, total, reach, slope, full):
    portions = [(1 << 20) // math.isqrt(rank ** slope) + 1 for rank in range(1, number_of + 1)]
    largest = reach if full else min(reach, max(-(-total // number_of), total * portions[0] // sum(portions)))
    least = 1 if total - largest >= number_of - 1 else 0
    holding, surplus = [largest] + [least] * (number_of - 1), total - largest - least * (number_of - 1)
    while surplus > 0:
        movable = [i for i in range(1, number_of) if holding[i] < largest] or [i for i in range(1, number_of) if holding[i] < reach]
        mass, remaining = sum([portions[i] for i in movable]), surplus
        for i in movable:
            addition = min(reach - holding[i], max(1, remaining * portions[i] // mass), surplus)
            holding[i] = holding[i] + addition
            surplus = surplus - addition
    return np.array(holding)


def normal_values(stream_key, shape, spread, limit, split=(), kind=jnp.bfloat16):
    values = jax.random.normal(stream_key, shape, jnp.float32) * spread
    if len(split) > 0:
        values = levels(stream_key, shape, split, -0.22, 0.18) * values
    return jnp.clip(values, min=-limit, max=limit).astype(kind)


def setup_inputs(seed: int = 0) -> dict:
    key_of = jax.random.split(jax.random.key(seed), 12)
    forward_start = normal_values(key_of[0], (SECTIONS, TOKENS, D), 1.0, 6.0, ((0, 8), (1, 32)))
    forward_feed = normal_values(key_of[1], (TICKS - 1, TOKENS, D), 1.0, 6.0, ((1, 32),))
    backward_start = normal_values(key_of[2], (SECTIONS, TOKENS, D), 1.0, 6.0, ((0, 8), (1, 32)))
    backward_feed = normal_values(key_of[3], (TICKS - 1, TOKENS, D), 1.0, 6.0, ((1, 32),))
    saved_inputs = normal_values(key_of[4], (SECTIONS, TICKS, TOKENS, D), 1.0, 6.0, ((0, 8), (2, 32)))
    expert_picks_keys = jax.random.split(jax.random.fold_in(key_of[5], 1), SECTIONS * TICKS * 2 * TOKENS // TOK_DEV)
    expert_picks_turns = jax.random.permutation(jax.random.fold_in(key_of[5], 3), SECTIONS * TICKS * 2 * TOKENS // TOK_DEV)
    expert_picks = jax.vmap(lambda own, number: shared_out(jax.random.fold_in(key_of[5], 2), own, number, TOK_DEV, EXPERTS, TOP, CAP, 2))(expert_picks_keys, expert_picks_turns).reshape((SECTIONS, TICKS, 2, TOKENS, TOP))
    pick_weights = jnp.clip(0.5 + 2.0 * jax.random.uniform(key_of[6], (SECTIONS, TICKS, 2, TOKENS, TOP), jnp.float32) ** levels(key_of[6], (SECTIONS, TICKS, 2, TOKENS, TOP), ((0, 8), (3, 32)), -0.2, 0.2), 0.5, 2.5)
    norm_gain = jnp.clip(1.0 + 0.16 * jax.random.normal(key_of[7], (SECTIONS, D), jnp.float32), 0.19921875, 1.796875).astype(jnp.bfloat16)
    w_gate = normal_values(key_of[8], (SECTIONS, D, EXPERTS * FF), D ** -0.5, 0.09375, ((0, 8), (2, 32)))
    w_up = normal_values(key_of[9], (SECTIONS, D, EXPERTS * FF), D ** -0.5, 0.09375, ((0, 8), (2, 32)))
    w_down = normal_values(key_of[10], (SECTIONS, EXPERTS * FF, D), FF ** -0.5, 0.1875, ((0, 8), (1, 32)))
    return dict(forward_start=forward_start, forward_feed=forward_feed, backward_start=backward_start, backward_feed=backward_feed, saved_inputs=saved_inputs, expert_picks=expert_picks, pick_weights=pick_weights, norm_gain=norm_gain, w_gate=w_gate, w_up=w_up, w_down=w_down)


EPSILON = 1e-06

def normalize(token_rows, gain_row):
    widened = token_rows.astype(jnp.float32)
    inverse = lax.rsqrt(lax.optimization_barrier(jnp.mean(widened * widened, axis=-1, keepdims=True)) + EPSILON)
    normed = (widened * inverse * gain_row.astype(jnp.float32)).astype(jnp.bfloat16)
    return (widened, inverse, normed)

def place_pairs(pair_picks):
    flat_picks = pair_picks.reshape(N_EXPERT, TOK_DEV * TOP).astype(jnp.int32)
    onehot = (flat_picks[:, :, None] == jnp.arange(EXPERTS, dtype=jnp.int32)[None, None, :]).astype(jnp.int32)
    before = jnp.cumsum(onehot, axis=1) - onehot
    slot_rank = lax.optimization_barrier(jnp.sum(before * onehot, axis=2)).astype(jnp.int32)
    source = jnp.arange(N_EXPERT, dtype=jnp.int32)[:, None]
    position = (source * CAP + slot_rank).astype(jnp.int32)
    return (flat_picks.reshape(-1), position.reshape(-1))

def split_experts(gate_w, up_w, down_w):
    gate_stack = gate_w.reshape(D, EXPERTS, FF).transpose(1, 0, 2)
    up_stack = up_w.reshape(D, EXPERTS, FF).transpose(1, 0, 2)
    down_stack = down_w.reshape(EXPERTS, FF, D)
    return (gate_stack, up_stack, down_stack)

def merge_members(member_parts):
    rounded = member_parts.astype(jnp.bfloat16)
    rounded = lax.optimization_barrier(rounded)
    return lax.optimization_barrier(jnp.sum(rounded.astype(jnp.float32), axis=1))

def expert_forward(bundle):
    token_rows, gate_w, up_w, down_w = bundle
    gate_act = jnp.dot(token_rows, gate_w, preferred_element_type=jnp.float32)
    up_act = jnp.dot(token_rows, up_w, preferred_element_type=jnp.float32)
    hidden = (jax.nn.silu(gate_act) * up_act).astype(jnp.bfloat16)
    hidden = lax.optimization_barrier(hidden)
    member_parts = jnp.einsum('mgf,gfd->mgd', hidden.reshape(-1, GROUP, FF_SH).astype(jnp.float32), down_w.reshape(GROUP, FF_SH, D).astype(jnp.float32))
    return merge_members(member_parts)

def expert_backward(bundle):
    token_rows, grad_rows, gate_w, up_w, down_w = bundle
    gate_act = jnp.dot(token_rows, gate_w, preferred_element_type=jnp.float32)
    up_act = jnp.dot(token_rows, up_w, preferred_element_type=jnp.float32)
    grad_hidden = jnp.dot(grad_rows, down_w.T, preferred_element_type=jnp.float32)
    sigmoid_gate = jax.nn.sigmoid(gate_act)
    grad_gate = (grad_hidden * up_act * sigmoid_gate * (1.0 + gate_act * (1.0 - sigmoid_gate))).astype(jnp.bfloat16)
    grad_up = (grad_hidden * (gate_act * sigmoid_gate)).astype(jnp.bfloat16)
    grad_gate = lax.optimization_barrier(grad_gate)
    grad_up = lax.optimization_barrier(grad_up)
    member_parts = jnp.einsum('mgf,dgf->mgd', grad_gate.reshape(-1, GROUP, FF_SH).astype(jnp.float32), gate_w.reshape(D, GROUP, FF_SH).astype(jnp.float32))
    member_parts = member_parts + jnp.einsum('mgf,dgf->mgd', grad_up.reshape(-1, GROUP, FF_SH).astype(jnp.float32), up_w.reshape(D, GROUP, FF_SH).astype(jnp.float32))
    return merge_members(member_parts)

def fill_buffers(pair_rows, expert_of, position):
    empty = jnp.zeros((EXPERTS, N_EXPERT * CAP, D), jnp.bfloat16)
    return empty.at[expert_of, position].set(pair_rows)

def moe_forward(bundle):
    token_rows, pair_picks, weights, gain_row, gate_w, up_w, down_w = bundle
    widened, inverse, normed = normalize(token_rows, gain_row)
    expert_of, position = place_pairs(pair_picks)
    buffers = fill_buffers(jnp.repeat(normed, TOP, axis=0), expert_of, position)
    gate_stack, up_stack, down_stack = split_experts(gate_w, up_w, down_w)
    outputs = lax.map(expert_forward, (buffers, gate_stack, up_stack, down_stack))
    per_pair = outputs[expert_of, position].reshape(TOKENS, TOP, D)
    mixed = widened + lax.optimization_barrier(jnp.sum(weights[:, :, None] * per_pair, axis=1))
    return mixed.astype(jnp.bfloat16)

def moe_backward(bundle):
    stored, grad_rows, pair_picks, weights, gain_row, gate_w, up_w, down_w = bundle
    widened, inverse, normed = normalize(stored, gain_row)
    expert_of, position = place_pairs(pair_picks)
    scaled = (weights[:, :, None] * grad_rows.astype(jnp.float32)[:, None, :]).astype(jnp.bfloat16).reshape(TOKENS * TOP, D)
    row_buffers = fill_buffers(jnp.repeat(normed, TOP, axis=0), expert_of, position)
    grad_buffers = fill_buffers(scaled, expert_of, position)
    gate_stack, up_stack, down_stack = split_experts(gate_w, up_w, down_w)
    outputs = lax.map(expert_backward, (row_buffers, grad_buffers, gate_stack, up_stack, down_stack))
    grad_normed = lax.optimization_barrier(jnp.sum(outputs[expert_of, position].reshape(TOKENS, TOP, D), axis=1))
    scaled_grad = grad_normed * gain_row.astype(jnp.float32)
    cubed = inverse * inverse * inverse
    grad_input = inverse * scaled_grad - widened * cubed * lax.optimization_barrier(jnp.mean(widened * scaled_grad, axis=-1, keepdims=True))
    return (grad_rows.astype(jnp.float32) + grad_input).astype(jnp.bfloat16)

def reference(forward_start, forward_feed, backward_start, backward_feed, saved_inputs, expert_picks, pick_weights, norm_gain, w_gate, w_up, w_down):
    forward_now = forward_start
    backward_now = backward_start
    forward_list = []
    backward_list = []
    for tick_index in range(TICKS):
        layer_out = lax.map(moe_forward, (forward_now, expert_picks[:, tick_index, 0], pick_weights[:, tick_index, 0], norm_gain, w_gate, w_up, w_down))
        grad_out = lax.map(moe_backward, (saved_inputs[:, tick_index], backward_now, expert_picks[:, tick_index, 1], pick_weights[:, tick_index, 1], norm_gain, w_gate, w_up, w_down))
        forward_list.append(layer_out)
        backward_list.append(grad_out)
        if tick_index + 1 < TICKS:
            forward_now = jnp.concatenate([forward_feed[tick_index][None], layer_out[:-1]], axis=0)
            backward_now = jnp.concatenate([grad_out[1:], backward_feed[tick_index][None]], axis=0)
    return (jnp.stack(forward_list, axis=1), jnp.stack(backward_list, axis=1))
```

```python
import jax
import jax.numpy as jnp
from jax import lax
from jax.sharding import PartitionSpec as P

EPSILON = 1e-06
EXPERTS = 8
CAP = 8


def from_behind(block, axis, distance):
    devices = range(lax.axis_size(axis))
    route = [(i - distance, i) for i in devices if i - distance in devices]
    return lax.ppermute(block, axis, route)


def y_shift(block, distance):
    return lax.ppermute(block, "expert", [(i, (i + 8 * distance) % 32) for i in range(32)])


def swap(block, bit):
    return lax.ppermute(block, "expert", [(i, i ^ bit) for i in range(32)])


def swap_half(block):
    return swap(block, 4)


def swap_pair(block):
    return swap(block, 2)


def swap_core(block):
    return swap(block, 1)


def local(
    forward_start,
    forward_feed,
    backward_start,
    backward_feed,
    saved_inputs,
    expert_picks,
    pick_weights,
    norm_gain,
    w_gate,
    w_up,
    w_down,
):
    tok_rows = forward_start.shape[1]
    model_width = forward_start.shape[2]
    tick_count = saved_inputs.shape[1]
    section_pos = lax.axis_index("section")
    section_count = lax.axis_size("section")
    expert_pos = lax.axis_index("expert")
    my_y = expert_pos // 8
    my_half = (expert_pos // 4) % 2
    gain_row = norm_gain[0].astype(jnp.float32)
    gate_w = w_gate[0]
    up_w = w_up[0]
    down_w = w_down[0]
    contract_dims = (((1,), (1,)), ((), ()))

    def normalize(token_rows):
        widened = token_rows.astype(jnp.float32)
        inverse = lax.rsqrt(jnp.mean(widened * widened, axis=-1, keepdims=True) + EPSILON)
        normed = (widened * inverse * gain_row).astype(jnp.bfloat16)
        return (widened, inverse, normed)

    def slot_table(pair_picks):
        flat_picks = pair_picks.reshape(-1)
        onehot = (flat_picks[:, None] == jnp.arange(EXPERTS, dtype=jnp.int32)[None, :]).astype(
            jnp.int32
        )
        before = jnp.cumsum(onehot, axis=0) - onehot
        rank = jnp.sum(before * onehot, axis=1)
        distance = (flat_picks // 2 - my_y + 4) % 4
        other = (flat_picks % 2) ^ my_half
        slots = (distance * 2 + other) * CAP + rank
        return (
            slots[:, None] == jnp.arange(EXPERTS * CAP, dtype=jnp.int32)[None, :]
        ).astype(jnp.bfloat16)

    def send_rows(stacked, placement):
        count = stacked.shape[0]
        buffer = jnp.einsum(
            "ps,kpd->ksd", placement, stacked, preferred_element_type=jnp.float32
        ).astype(jnp.bfloat16)
        buffer = buffer.reshape(count, 4, 2 * CAP, model_width)
        arrived = [buffer[:, 0]] + [y_shift(buffer[:, d], d) for d in (1, 2, 3)]
        arrived = jnp.stack(arrived, axis=1).reshape(count, 4, 2, CAP, model_width)
        kept = arrived[:, :, 0].reshape(count, 4 * CAP, model_width)
        swapped = swap_half(arrived[:, :, 1].reshape(count, 4 * CAP, model_width))
        own = jnp.concatenate([kept, swapped], axis=1)
        pair = jnp.concatenate([own, swap_pair(own)], axis=1)
        return jnp.concatenate([pair, swap_core(pair)], axis=1)

    def add(left, right):
        return (left.astype(jnp.float32) + right.astype(jnp.float32)).astype(jnp.bfloat16)

    def return_sums(partial):
        pair = add(partial[:128], swap_core(partial[128:]))
        own = add(pair[:64], swap_pair(pair[64:]))
        kept = own[:32].reshape(4, CAP, model_width)
        swapped = swap_half(own[32:]).reshape(4, CAP, model_width)
        both = jnp.stack([kept, swapped], axis=1).reshape(4, 2 * CAP, model_width)
        back = [both[0]] + [y_shift(both[d], -d) for d in (1, 2, 3)]
        return jnp.concatenate(back, axis=0)

    def pick_rows(placement, sums):
        return jnp.dot(placement, sums, preferred_element_type=jnp.float32)

    def expert_forward(token_rows):
        gate_act = jnp.dot(token_rows, gate_w, preferred_element_type=jnp.float32)
        up_act = jnp.dot(token_rows, up_w, preferred_element_type=jnp.float32)
        hidden = (jax.nn.silu(gate_act) * up_act).astype(jnp.bfloat16)
        return jnp.dot(hidden, down_w, preferred_element_type=jnp.float32).astype(jnp.bfloat16)

    def expert_backward(token_rows, grad_rows):
        gate_act = jnp.dot(token_rows, gate_w, preferred_element_type=jnp.float32)
        up_act = jnp.dot(token_rows, up_w, preferred_element_type=jnp.float32)
        grad_hidden = lax.dot_general(
            grad_rows, down_w, contract_dims, preferred_element_type=jnp.float32
        )
        sigmoid_gate = jax.nn.sigmoid(gate_act)
        grad_gate = (
            grad_hidden * up_act * sigmoid_gate * (1.0 + gate_act * (1.0 - sigmoid_gate))
        ).astype(jnp.bfloat16)
        grad_up = (grad_hidden * (gate_act * sigmoid_gate)).astype(jnp.bfloat16)
        member_grad = lax.dot_general(
            grad_gate, gate_w, contract_dims, preferred_element_type=jnp.float32
        )
        member_grad = member_grad + lax.dot_general(
            grad_up, up_w, contract_dims, preferred_element_type=jnp.float32
        )
        return member_grad.astype(jnp.bfloat16)

    forward_now = forward_start[0]
    backward_now = backward_start[0]
    forward_list = []
    backward_list = []
    for tick_index in range(tick_count):
        widened, inverse, normed = normalize(forward_now)
        placement = slot_table(expert_picks[0, tick_index, 0])
        received = send_rows(normed[None], placement)
        sums = return_sums(expert_forward(received[0]))
        layer_out = (
            widened + pick_weights[0, tick_index, 0] * pick_rows(placement, sums)
        ).astype(jnp.bfloat16)
        stored_wide, stored_inverse, stored_normed = normalize(saved_inputs[0, tick_index])
        back_placement = slot_table(expert_picks[0, tick_index, 1])
        scaled = (
            pick_weights[0, tick_index, 1] * backward_now.astype(jnp.float32)
        ).astype(jnp.bfloat16)
        received_back = send_rows(jnp.stack([stored_normed, scaled]), back_placement)
        grad_sums = return_sums(expert_backward(received_back[0], received_back[1]))
        scaled_grad = pick_rows(back_placement, grad_sums) * gain_row
        cubed = stored_inverse * stored_inverse * stored_inverse
        grad_input = stored_inverse * scaled_grad - stored_wide * cubed * jnp.mean(
            stored_wide * scaled_grad, axis=-1, keepdims=True
        )
        grad_out = (backward_now.astype(jnp.float32) + grad_input).astype(jnp.bfloat16)
        forward_list.append(layer_out)
        backward_list.append(grad_out)
        if tick_index + 1 < tick_count:
            arrived = from_behind(layer_out, "section", 1)
            forward_now = jnp.where(section_pos == 0, forward_feed[tick_index], arrived)
            returned = from_behind(grad_out, "section", -1)
            backward_now = jnp.where(
                section_pos == section_count - 1, backward_feed[tick_index], returned
            )
    return (jnp.stack(forward_list)[None], jnp.stack(backward_list)[None])


def solution(mesh):
    in_specs = (
        P("section", "expert", None),
        P(None, "expert", None),
        P("section", "expert", None),
        P(None, "expert", None),
        P("section", None, "expert", None),
        P("section", None, None, "expert", None),
        P("section", None, None, "expert", None),
        P("section", None),
        P("section", None, "expert"),
        P("section", None, "expert"),
        P("section", "expert", None),
    )
    out_specs = (P("section", None, "expert", None), P("section", None, "expert", None))
    return jax.shard_map(local, mesh=mesh, in_specs=in_specs, out_specs=out_specs, check_vma=False)
```

```python
import jax
import jax.numpy as jnp
from jax import lax
from jax.experimental import pallas as pl
from jax.experimental.pallas import tpu as pltpu
from jax.sharding import PartitionSpec as P

TILE = 512
NT = (((1,), (1,)), ((), ()))


def dot32(left, right):
    return jnp.dot(left, right, preferred_element_type=jnp.float32)


def dot_nt(left, right):
    return lax.dot_general(left, right, NT, preferred_element_type=jnp.float32)


def forward_kernel(pair_ref, core_ref, gate_ref, up_ref, down_ref, keep_ref, send_ref,
                   x_buf, gate_buf, up_buf, down_buf, sems):
    half, width = pair_ref.shape
    tiles = width // TILE
    rows = [
        pltpu.make_async_copy(pair_ref, x_buf.at[:half], sems.at[0]),
        pltpu.make_async_copy(core_ref, x_buf.at[half:], sems.at[1]),
    ]
    weights = [
        pltpu.make_async_copy(gate_ref, gate_buf, sems.at[2]),
        pltpu.make_async_copy(up_ref, up_buf, sems.at[3]),
        pltpu.make_async_copy(down_ref, down_buf, sems.at[4]),
    ]
    for copy in rows + weights:
        copy.start()
    for copy in rows + weights[:1]:
        copy.wait()
    gate = dot32(x_buf[...], gate_buf[...])
    weights[1].wait()
    up = dot32(x_buf[...], up_buf[...])
    hidden = (gate * jax.nn.sigmoid(gate) * up).astype(jnp.bfloat16)
    weights[2].wait()
    for t in range(tiles):
        part = pl.ds(t * TILE, TILE)
        out = dot32(hidden, down_buf[:, part]).astype(jnp.bfloat16)
        keep_ref[:, part] = out[:half]
        send_ref[:, part] = out[half:]


def gate_up_kernel(pair_ref, core_ref, gate_ref, up_ref, g_ref, u_ref, x_buf, gate_buf, up_buf, sems):
    half = pair_ref.shape[0]
    rows = [
        pltpu.make_async_copy(pair_ref, x_buf.at[:half], sems.at[0]),
        pltpu.make_async_copy(core_ref, x_buf.at[half:], sems.at[1]),
    ]
    weights = [
        pltpu.make_async_copy(gate_ref, gate_buf, sems.at[2]),
        pltpu.make_async_copy(up_ref, up_buf, sems.at[3]),
    ]
    for copy in rows + weights:
        copy.start()
    for copy in rows + weights[:1]:
        copy.wait()
    g_ref[...] = dot32(x_buf[...], gate_buf[...])
    weights[1].wait()
    u_ref[...] = dot32(x_buf[...], up_buf[...])


def backward_kernel(g_ref, u_ref, pair_ref, core_ref, gate_ref, up_ref, down_ref, keep_ref, send_ref,
                    x_buf, gate_buf, up_buf, down_buf, sems):
    half, width = pair_ref.shape
    tiles = width // TILE
    rows = [
        pltpu.make_async_copy(pair_ref, x_buf.at[:half], sems.at[0]),
        pltpu.make_async_copy(core_ref, x_buf.at[half:], sems.at[1]),
    ]
    weights = [
        pltpu.make_async_copy(down_ref, down_buf, sems.at[4]),
        pltpu.make_async_copy(gate_ref, gate_buf, sems.at[2]),
        pltpu.make_async_copy(up_ref, up_buf, sems.at[3]),
    ]
    for copy in rows + weights:
        copy.start()
    for copy in rows + weights[:1]:
        copy.wait()
    grad_hidden = dot_nt(x_buf[...], down_buf[...])
    gate, up = g_ref[...], u_ref[...]
    sigmoid = jax.nn.sigmoid(gate)
    grad_gate = (grad_hidden * up * sigmoid * (1.0 + gate * (1.0 - sigmoid))).astype(jnp.bfloat16)
    grad_up = (grad_hidden * (gate * sigmoid)).astype(jnp.bfloat16)
    weights[1].wait()
    weights[2].wait()
    for t in range(tiles):
        part = pl.ds(t * TILE, TILE)
        out = dot_nt(grad_gate, gate_buf[part, :]) + dot_nt(grad_up, up_buf[part, :])
        out = out.astype(jnp.bfloat16)
        keep_ref[:, part] = out[:half]
        send_ref[:, part] = out[half:]


def _call(kernel, operands, n_vmem, outs, scratch, flops, nbytes):
    anywhere = pl.BlockSpec(memory_space=pl.ANY)
    vmem = pl.BlockSpec(memory_space=pltpu.VMEM)
    return pl.pallas_call(
        kernel,
        out_shape=outs,
        in_specs=[vmem] * n_vmem + [anywhere] * (len(operands) - n_vmem),
        out_specs=[vmem] * len(outs),
        scratch_shapes=scratch,
        compiler_params=pltpu.CompilerParams(vmem_limit_bytes=24 * 1024 * 1024),
        cost_estimate=pl.CostEstimate(flops=flops, bytes_accessed=nbytes, transcendentals=0),
    )(*operands)


def expert_forward(pair, core, gate_w, up_w, down_w):
    half, width = pair.shape
    hidden = gate_w.shape[1]
    bf = jnp.bfloat16
    outs = [jax.ShapeDtypeStruct((half, width), bf)] * 2
    scratch = [pltpu.VMEM((2 * half, width), bf), pltpu.VMEM((width, hidden), bf), pltpu.VMEM((width, hidden), bf),
               pltpu.VMEM((hidden, width), bf), pltpu.SemaphoreType.DMA((5,))]
    return _call(forward_kernel, (pair, core, gate_w, up_w, down_w), 0, outs, scratch, 12 * half * width * hidden, 3 * width * hidden * 2 + 8 * half * width)


def expert_gate_up(pair, core, gate_w, up_w):
    half, width = pair.shape
    hidden = gate_w.shape[1]
    bf = jnp.bfloat16
    outs = [jax.ShapeDtypeStruct((2 * half, hidden), jnp.float32)] * 2
    scratch = [pltpu.VMEM((2 * half, width), bf), pltpu.VMEM((width, hidden), bf), pltpu.VMEM((width, hidden), bf),
               pltpu.SemaphoreType.DMA((4,))]
    return _call(gate_up_kernel, (pair, core, gate_w, up_w), 0, outs, scratch, 8 * half * width * hidden, 2 * width * hidden * 2 + 4 * half * width)


def expert_backward(gate, up, pair, core, gate_w, up_w, down_w):
    half, width = pair.shape
    hidden = gate_w.shape[1]
    bf = jnp.bfloat16
    outs = [jax.ShapeDtypeStruct((half, width), bf)] * 2
    scratch = [pltpu.VMEM((2 * half, width), bf), pltpu.VMEM((width, hidden), bf), pltpu.VMEM((width, hidden), bf),
               pltpu.VMEM((hidden, width), bf), pltpu.SemaphoreType.DMA((5,))]
    return _call(backward_kernel, (gate, up, pair, core, gate_w, up_w, down_w), 2, outs, scratch, 12 * half * width * hidden, 3 * width * hidden * 2 + 8 * half * width)


EPSILON = 1e-06
EXPERTS = 8
CAP = 8


def from_behind(block, axis, distance):
    devices = range(lax.axis_size(axis))
    route = [(i - distance, i) for i in devices if i - distance in devices]
    return lax.ppermute(block, axis, route)


def y_shift(block, distance):
    return lax.ppermute(block, "expert", [(i, (i + 8 * distance) % 32) for i in range(32)])


def swap(block, bit):
    return lax.ppermute(block, "expert", [(i, i ^ bit) for i in range(32)])


def swap_half(block):
    return swap(block, 4)


def swap_pair(block):
    return swap(block, 2)


def swap_core(block):
    return swap(block, 1)


def after(value, *others):
    tied = lax.optimization_barrier((value, *[other[:8, :128] for other in others]))
    return tied[0]


def add(left, right):
    return (left.astype(jnp.float32) + right.astype(jnp.float32)).astype(jnp.bfloat16)


def local(
    forward_start,
    forward_feed,
    backward_start,
    backward_feed,
    saved_inputs,
    expert_picks,
    pick_weights,
    norm_gain,
    w_gate,
    w_up,
    w_down,
):
    model_width = forward_start.shape[2]
    section_pos = lax.axis_index("section")
    section_count = lax.axis_size("section")
    expert_pos = lax.axis_index("expert")
    my_y = expert_pos // 8
    my_half = (expert_pos // 4) % 2
    gain_row = norm_gain[0].astype(jnp.float32)
    gate_w = w_gate[0]
    up_w = w_up[0]
    down_w = w_down[0]

    def normalize(token_rows):
        widened = token_rows.astype(jnp.float32)
        inverse = lax.rsqrt(jnp.mean(widened * widened, axis=-1, keepdims=True) + EPSILON)
        normed = (widened * inverse * gain_row).astype(jnp.bfloat16)
        return (widened, inverse, normed)

    def slot_table(pair_picks):
        flat_picks = pair_picks.reshape(-1)
        onehot = (flat_picks[:, None] == jnp.arange(EXPERTS, dtype=jnp.int32)[None, :]).astype(
            jnp.int32
        )
        before = jnp.cumsum(onehot, axis=0) - onehot
        rank = jnp.sum(before * onehot, axis=1)
        distance = (flat_picks // 2 - my_y + 4) % 4
        other = (flat_picks % 2) ^ my_half
        slots = (distance * 2 + other) * CAP + rank
        return (
            slots[:, None] == jnp.arange(EXPERTS * CAP, dtype=jnp.int32)[None, :]
        ).astype(jnp.bfloat16)

    def send_y(rows, placement):
        buffer = lax.dot_general(
            placement, rows, (((0,), (0,)), ((), ())), preferred_element_type=jnp.float32
        ).astype(jnp.bfloat16)
        slots = [buffer[16 * d : 16 * d + 16] for d in range(4)]
        return [slots[0]] + [y_shift(slots[d], d) for d in (1, 2, 3)]

    def split(arrived):
        kept = jnp.concatenate([a[:CAP] for a in arrived])
        crossing = jnp.concatenate([a[CAP:] for a in arrived])
        return kept, crossing

    def spread(kept, crossing):
        crossed = swap_half(crossing)
        pair = jnp.concatenate([kept, crossed, swap_pair(kept), swap_pair(crossed)])
        return pair, swap_core(pair)

    def gather_back(keep, send):
        pair = add(keep, swap_core(send))
        crossed = add(pair[32:64], swap_pair(pair[96:]))
        crossing = swap_half(crossed)
        kept = add(pair[:32], swap_pair(pair[64:96]))
        both = [
            jnp.concatenate([kept[CAP * d : CAP * d + CAP], crossing[CAP * d : CAP * d + CAP]])
            for d in range(4)
        ]
        return jnp.concatenate([both[0]] + [y_shift(both[d], -d) for d in (1, 2, 3)])

    def pick_rows(placement, sums):
        return jnp.dot(placement, sums, preferred_element_type=jnp.float32)

    def forward_send(rows, tick):
        widened, _, normed = normalize(rows)
        placement = slot_table(expert_picks[0, tick, 0])
        return widened, placement, send_y(normed, placement)

    def forward_end(widened, placement, sums, tick):
        return (widened + pick_weights[0, tick, 0] * pick_rows(placement, sums)).astype(
            jnp.bfloat16
        )

    def scale(rows, tick):
        return (pick_weights[0, tick, 1] * rows.astype(jnp.float32)).astype(jnp.bfloat16)

    def backward_end(saved, rows, placement, sums):
        wide, inverse = saved
        scaled_grad = pick_rows(placement, sums) * gain_row
        cubed = inverse * inverse * inverse
        grad_input = inverse * scaled_grad - wide * cubed * jnp.mean(
            wide * scaled_grad, axis=-1, keepdims=True
        )
        return (rows.astype(jnp.float32) + grad_input).astype(jnp.bfloat16)

    rows_f0, rows_g0 = forward_start[0], backward_start[0]
    wide_f0, place_f0, y_f0 = forward_send(rows_f0, 0)
    wide_s0, inv_s0, norm_s0 = normalize(saved_inputs[0, 0])
    place_b0 = slot_table(expert_picks[0, 0, 1])
    y_s0 = send_y(norm_s0, place_b0)
    y_g0 = send_y(scale(rows_g0, 0), place_b0)
    wide_s1, inv_s1, norm_s1 = normalize(saved_inputs[0, 1])
    place_b1 = slot_table(expert_picks[0, 1, 1])

    f0 = spread(*split(y_f0))
    s0 = spread(*split(y_s0))
    g0 = spread(*split(y_g0))
    rf0 = gather_back(*expert_forward(*f0, gate_w, up_w, down_w))
    act0 = expert_gate_up(*s0, gate_w, up_w)
    rg0 = gather_back(*expert_backward(*act0, *g0, gate_w, up_w, down_w))
    out_f0 = forward_end(wide_f0, place_f0, rf0, 0)
    rel_f = from_behind(out_f0, "section", 1)
    out_g0 = backward_end((wide_s0, inv_s0), rows_g0, place_b0, rg0)
    rel_g = from_behind(out_g0, "section", -1)

    y_s1 = send_y(norm_s1, place_b1)
    s1 = spread(*split(y_s1))
    act1 = expert_gate_up(*s1, gate_w, up_w)

    rows_f1 = jnp.where(section_pos == 0, forward_feed[0], rel_f)
    rows_g1 = jnp.where(section_pos == section_count - 1, backward_feed[0], rel_g)
    wide_f1, place_f1, y_f1 = forward_send(rows_f1, 1)
    f1 = spread(*split(y_f1))
    rf1 = gather_back(*expert_forward(*f1, gate_w, up_w, down_w))
    out_f1 = forward_end(wide_f1, place_f1, rf1, 1)
    y_g1 = send_y(scale(rows_g1, 1), place_b1)
    g1 = spread(*split(y_g1))
    rg1 = gather_back(*expert_backward(*act1, *g1, gate_w, up_w, down_w))
    out_g1 = backward_end((wide_s1, inv_s1), rows_g1, place_b1, rg1)
    return (jnp.stack([out_f0, out_f1])[None], jnp.stack([out_g0, out_g1])[None])


def solution(mesh):
    in_specs = (
        P("section", "expert", None),
        P(None, "expert", None),
        P("section", "expert", None),
        P(None, "expert", None),
        P("section", None, "expert", None),
        P("section", None, None, "expert", None),
        P("section", None, None, "expert", None),
        P("section", None),
        P("section", None, "expert"),
        P("section", None, "expert"),
        P("section", "expert", None),
    )
    out_specs = (P("section", None, "expert", None), P("section", None, "expert", None))
    return jax.shard_map(local, mesh=mesh, in_specs=in_specs, out_specs=out_specs, check_vma=False)
```

```python
import jax
import jax.numpy as jnp
from jax import lax
from jax.experimental import pallas as pl
from jax.experimental.pallas import tpu as pltpu
from jax.sharding import PartitionSpec as P

TILE = 512
NT = (((1,), (1,)), ((), ()))


def dot32(left, right):
    return jnp.dot(left, right, preferred_element_type=jnp.float32)


def dot_nt(left, right):
    return lax.dot_general(left, right, NT, preferred_element_type=jnp.float32)


def both(pair_ref, core_ref):
    return jnp.concatenate([pair_ref[...], core_ref[...]], axis=0)


def store(keep_ref, send_ref, part, out):
    half = keep_ref.shape[0]
    out = out.astype(jnp.bfloat16)
    keep_ref[:, part] = out[:half]
    send_ref[:, part] = out[half:]


def forward_kernel(pair_ref, core_ref, gate_ref, up_ref, down_ref, keep_ref, send_ref):
    rows = both(pair_ref, core_ref)
    gate = dot32(rows, gate_ref[...])
    up = dot32(rows, up_ref[...])
    hidden = (gate * jax.nn.sigmoid(gate) * up).astype(jnp.bfloat16)
    for t in range(keep_ref.shape[1] // TILE):
        part = pl.ds(t * TILE, TILE)
        store(keep_ref, send_ref, part, dot32(hidden, down_ref[:, part]))


def gate_up_kernel(pair_ref, core_ref, gate_ref, up_ref, g_ref, u_ref):
    rows = both(pair_ref, core_ref)
    g_ref[...] = dot32(rows, gate_ref[...])
    u_ref[...] = dot32(rows, up_ref[...])


def backward_kernel(g_ref, u_ref, pair_ref, core_ref, gate_ref, up_ref, down_ref, keep_ref, send_ref):
    grad_hidden = dot_nt(both(pair_ref, core_ref), down_ref[...])
    gate, up = g_ref[...], u_ref[...]
    sigmoid = jax.nn.sigmoid(gate)
    grad_gate = (grad_hidden * up * sigmoid * (1.0 + gate * (1.0 - sigmoid))).astype(jnp.bfloat16)
    grad_up = (grad_hidden * (gate * sigmoid)).astype(jnp.bfloat16)
    for t in range(keep_ref.shape[1] // TILE):
        part = pl.ds(t * TILE, TILE)
        store(
            keep_ref,
            send_ref,
            part,
            dot_nt(grad_gate, gate_ref[part, :]) + dot_nt(grad_up, up_ref[part, :]),
        )


def _call(kernel, operands, outs, flops, nbytes):
    vmem = pl.BlockSpec(memory_space=pltpu.VMEM)
    return pl.pallas_call(
        kernel,
        out_shape=outs,
        in_specs=[vmem] * len(operands),
        out_specs=[vmem] * len(outs),
        compiler_params=pltpu.CompilerParams(vmem_limit_bytes=24 * 1024 * 1024),
        cost_estimate=pl.CostEstimate(flops=flops, bytes_accessed=nbytes, transcendentals=0),
    )(*operands)


def expert_forward(pair, core, gate_w, up_w, down_w):
    half, width = pair.shape
    hidden = gate_w.shape[1]
    outs = [jax.ShapeDtypeStruct((half, width), jnp.bfloat16)] * 2
    return _call(forward_kernel, (pair, core, gate_w, up_w, down_w), outs,
                 12 * half * width * hidden, 6 * width * hidden + 8 * half * width)


def expert_gate_up(pair, core, gate_w, up_w):
    half, width = pair.shape
    hidden = gate_w.shape[1]
    outs = [jax.ShapeDtypeStruct((2 * half, hidden), jnp.float32)] * 2
    return _call(gate_up_kernel, (pair, core, gate_w, up_w), outs,
                 8 * half * width * hidden, 4 * width * hidden + 4 * half * width)


def expert_backward(gate, up, pair, core, gate_w, up_w, down_w):
    half, width = pair.shape
    hidden = gate_w.shape[1]
    outs = [jax.ShapeDtypeStruct((half, width), jnp.bfloat16)] * 2
    return _call(backward_kernel, (gate, up, pair, core, gate_w, up_w, down_w), outs,
                 12 * half * width * hidden, 6 * width * hidden + 8 * half * width)


EPSILON = 1e-06
EXPERTS = 8
CAP = 8


def from_behind(block, axis, distance):
    devices = range(lax.axis_size(axis))
    route = [(i - distance, i) for i in devices if i - distance in devices]
    return lax.ppermute(block, axis, route)


def y_shift(block, distance):
    return lax.ppermute(block, "expert", [(i, (i + 8 * distance) % 32) for i in range(32)])


def swap(block, bit):
    return lax.ppermute(block, "expert", [(i, i ^ bit) for i in range(32)])


def swap_half(block):
    return swap(block, 4)


def swap_pair(block):
    return swap(block, 2)


def swap_core(block):
    return swap(block, 1)


def add(left, right):
    return (left.astype(jnp.float32) + right.astype(jnp.float32)).astype(jnp.bfloat16)


def local(
    forward_start,
    forward_feed,
    backward_start,
    backward_feed,
    saved_inputs,
    expert_picks,
    pick_weights,
    norm_gain,
    w_gate,
    w_up,
    w_down,
):
    model_width = forward_start.shape[2]
    section_pos = lax.axis_index("section")
    section_count = lax.axis_size("section")
    expert_pos = lax.axis_index("expert")
    my_y = expert_pos // 8
    my_half = (expert_pos // 4) % 2
    gain_row = norm_gain[0].astype(jnp.float32)
    gate_w = w_gate[0]
    up_w = w_up[0]
    down_w = w_down[0]

    def normalize(token_rows):
        widened = token_rows.astype(jnp.float32)
        inverse = lax.rsqrt(jnp.mean(widened * widened, axis=-1, keepdims=True) + EPSILON)
        normed = (widened * inverse * gain_row).astype(jnp.bfloat16)
        return (widened, inverse, normed)

    def slot_table(pair_picks):
        flat_picks = pair_picks.reshape(-1)
        onehot = (flat_picks[:, None] == jnp.arange(EXPERTS, dtype=jnp.int32)[None, :]).astype(
            jnp.int32
        )
        before = jnp.cumsum(onehot, axis=0) - onehot
        rank = jnp.sum(before * onehot, axis=1)
        distance = (flat_picks // 2 - my_y + 4) % 4
        other = (flat_picks % 2) ^ my_half
        slots = (distance * 2 + other) * CAP + rank
        return (
            slots[:, None] == jnp.arange(EXPERTS * CAP, dtype=jnp.int32)[None, :]
        ).astype(jnp.bfloat16)

    def send_y(rows, placement):
        buffer = lax.dot_general(
            placement, rows, (((0,), (0,)), ((), ())), preferred_element_type=jnp.float32
        ).astype(jnp.bfloat16)
        slots = [buffer[16 * d : 16 * d + 16] for d in range(4)]
        return [slots[0]] + [y_shift(slots[d], d) for d in (1, 2, 3)]

    def split(arrived):
        kept = jnp.concatenate([a[:CAP] for a in arrived])
        crossing = jnp.concatenate([a[CAP:] for a in arrived])
        return kept, crossing

    def spread(kept, crossing):
        crossed = swap_half(crossing)
        pair = jnp.concatenate([kept, crossed, swap_pair(kept), swap_pair(crossed)])
        return pair, swap_core(pair)

    def gather_back(keep, send):
        pair = add(keep, swap_core(send))
        crossed = add(pair[32:64], swap_pair(pair[96:]))
        crossing = swap_half(crossed)
        kept = add(pair[:32], swap_pair(pair[64:96]))
        both = [
            jnp.concatenate([kept[CAP * d : CAP * d + CAP], crossing[CAP * d : CAP * d + CAP]])
            for d in range(4)
        ]
        return jnp.concatenate([both[0]] + [y_shift(both[d], -d) for d in (1, 2, 3)])

    def pick_rows(placement, sums):
        return jnp.dot(placement, sums, preferred_element_type=jnp.float32)

    def forward_send(rows, tick):
        widened, _, normed = normalize(rows)
        placement = slot_table(expert_picks[0, tick, 0])
        return widened, placement, send_y(normed, placement)

    def forward_end(widened, placement, sums, tick):
        return (widened + pick_weights[0, tick, 0] * pick_rows(placement, sums)).astype(
            jnp.bfloat16
        )

    def scale(rows, tick):
        return (pick_weights[0, tick, 1] * rows.astype(jnp.float32)).astype(jnp.bfloat16)

    def backward_end(saved, rows, placement, sums):
        wide, inverse = saved
        scaled_grad = pick_rows(placement, sums) * gain_row
        cubed = inverse * inverse * inverse
        grad_input = inverse * scaled_grad - wide * cubed * jnp.mean(
            wide * scaled_grad, axis=-1, keepdims=True
        )
        return (rows.astype(jnp.float32) + grad_input).astype(jnp.bfloat16)

    rows_f0, rows_g0 = forward_start[0], backward_start[0]
    wide_f0, place_f0, y_f0 = forward_send(rows_f0, 0)
    wide_s0, inv_s0, norm_s0 = normalize(saved_inputs[0, 0])
    place_b0 = slot_table(expert_picks[0, 0, 1])
    y_s0 = send_y(norm_s0, place_b0)
    y_g0 = send_y(scale(rows_g0, 0), place_b0)
    wide_s1, inv_s1, norm_s1 = normalize(saved_inputs[0, 1])
    place_b1 = slot_table(expert_picks[0, 1, 1])

    f0 = spread(*split(y_f0))
    s0 = spread(*split(y_s0))
    g0 = spread(*split(y_g0))
    rf0 = gather_back(*expert_forward(*f0, gate_w, up_w, down_w))
    act0 = expert_gate_up(*s0, gate_w, up_w)
    rg0 = gather_back(*expert_backward(*act0, *g0, gate_w, up_w, down_w))
    out_f0 = forward_end(wide_f0, place_f0, rf0, 0)
    rel_f = from_behind(out_f0, "section", 1)
    out_g0 = backward_end((wide_s0, inv_s0), rows_g0, place_b0, rg0)
    rel_g = from_behind(out_g0, "section", -1)

    y_s1 = send_y(norm_s1, place_b1)
    s1 = spread(*split(y_s1))
    act1 = expert_gate_up(*s1, gate_w, up_w)

    rows_f1 = jnp.where(section_pos == 0, forward_feed[0], rel_f)
    rows_g1 = jnp.where(section_pos == section_count - 1, backward_feed[0], rel_g)
    wide_f1, place_f1, y_f1 = forward_send(rows_f1, 1)
    f1 = spread(*split(y_f1))
    rf1 = gather_back(*expert_forward(*f1, gate_w, up_w, down_w))
    out_f1 = forward_end(wide_f1, place_f1, rf1, 1)
    y_g1 = send_y(scale(rows_g1, 1), place_b1)
    g1 = spread(*split(y_g1))
    rg1 = gather_back(*expert_backward(*act1, *g1, gate_w, up_w, down_w))
    out_g1 = backward_end((wide_s1, inv_s1), rows_g1, place_b1, rg1)
    return (jnp.stack([out_f0, out_f1])[None], jnp.stack([out_g0, out_g1])[None])


def solution(mesh):
    in_specs = (
        P("section", "expert", None),
        P(None, "expert", None),
        P("section", "expert", None),
        P(None, "expert", None),
        P("section", None, "expert", None),
        P("section", None, None, "expert", None),
        P("section", None, None, "expert", None),
        P("section", None),
        P("section", None, "expert"),
        P("section", None, "expert"),
        P("section", "expert", None),
    )
    out_specs = (P("section", None, "expert", None), P("section", None, "expert", None))
    return jax.shard_map(local, mesh=mesh, in_specs=in_specs, out_specs=out_specs, check_vma=False)
```

```python
import jax
import jax.numpy as jnp
from jax import lax
from jax.experimental import pallas as pl
from jax.experimental.pallas import tpu as pltpu
from jax.sharding import PartitionSpec as P

TILE = 512
NT = (((1,), (1,)), ((), ()))


def dot32(left, right):
    return jnp.dot(left, right, preferred_element_type=jnp.float32)


def dot_nt(left, right):
    return lax.dot_general(left, right, NT, preferred_element_type=jnp.float32)


def both(pair_ref, core_ref):
    return jnp.concatenate([pair_ref[...], core_ref[...]], axis=0)


def store(keep_ref, send_ref, part, out):
    half = keep_ref.shape[0]
    out = out.astype(jnp.bfloat16)
    keep_ref[:, part] = out[:half]
    send_ref[:, part] = out[half:]


def forward_kernel(pair_ref, core_ref, gate_ref, up_ref, down_ref, keep_ref, send_ref):
    rows = both(pair_ref, core_ref)
    gate = dot32(rows, gate_ref[...])
    up = dot32(rows, up_ref[...])
    hidden = (gate * jax.nn.sigmoid(gate) * up).astype(jnp.bfloat16)
    for t in range(keep_ref.shape[1] // TILE):
        part = pl.ds(t * TILE, TILE)
        store(keep_ref, send_ref, part, dot32(hidden, down_ref[:, part]))


def gate_up_kernel(pair_ref, core_ref, gate_ref, up_ref, g_ref, u_ref):
    rows = both(pair_ref, core_ref)
    g_ref[...] = dot32(rows, gate_ref[...])
    u_ref[...] = dot32(rows, up_ref[...])


def backward_kernel(g_ref, u_ref, pair_ref, core_ref, gate_ref, up_ref, down_ref, keep_ref, send_ref):
    grad_hidden = dot_nt(both(pair_ref, core_ref), down_ref[...])
    gate, up = g_ref[...], u_ref[...]
    sigmoid = jax.nn.sigmoid(gate)
    grad_gate = (grad_hidden * up * sigmoid * (1.0 + gate * (1.0 - sigmoid))).astype(jnp.bfloat16)
    grad_up = (grad_hidden * (gate * sigmoid)).astype(jnp.bfloat16)
    for t in range(keep_ref.shape[1] // TILE):
        part = pl.ds(t * TILE, TILE)
        store(
            keep_ref,
            send_ref,
            part,
            dot_nt(grad_gate, gate_ref[part, :]) + dot_nt(grad_up, up_ref[part, :]),
        )


def _call(kernel, operands, outs, flops, nbytes):
    vmem = pl.BlockSpec(memory_space=pltpu.VMEM)
    return pl.pallas_call(
        kernel,
        out_shape=outs,
        in_specs=[vmem] * len(operands),
        out_specs=[vmem] * len(outs),
        compiler_params=pltpu.CompilerParams(vmem_limit_bytes=10 * 1024 * 1024),
        cost_estimate=pl.CostEstimate(flops=flops, bytes_accessed=nbytes, transcendentals=0),
    )(*operands)


def expert_forward(pair, core, gate_w, up_w, down_w):
    half, width = pair.shape
    hidden = gate_w.shape[1]
    outs = [jax.ShapeDtypeStruct((half, width), jnp.bfloat16)] * 2
    return _call(forward_kernel, (pair, core, gate_w, up_w, down_w), outs,
                 12 * half * width * hidden, 6 * width * hidden + 8 * half * width)


def expert_gate_up(pair, core, gate_w, up_w):
    half, width = pair.shape
    hidden = gate_w.shape[1]
    outs = [jax.ShapeDtypeStruct((2 * half, hidden), jnp.float32)] * 2
    return _call(gate_up_kernel, (pair, core, gate_w, up_w), outs,
                 8 * half * width * hidden, 4 * width * hidden + 4 * half * width)


def expert_backward(gate, up, pair, core, gate_w, up_w, down_w):
    half, width = pair.shape
    hidden = gate_w.shape[1]
    outs = [jax.ShapeDtypeStruct((half, width), jnp.bfloat16)] * 2
    return _call(backward_kernel, (gate, up, pair, core, gate_w, up_w, down_w), outs,
                 12 * half * width * hidden, 6 * width * hidden + 8 * half * width)


EPSILON = 1e-06
EXPERTS = 8
CAP = 8


def from_behind(block, axis, distance):
    devices = range(lax.axis_size(axis))
    route = [(i - distance, i) for i in devices if i - distance in devices]
    return lax.ppermute(block, axis, route)


def y_shift(block, distance):
    return lax.ppermute(block, "expert", [(i, (i + 8 * distance) % 32) for i in range(32)])


def swap(block, bit):
    return lax.ppermute(block, "expert", [(i, i ^ bit) for i in range(32)])


def swap_half(block):
    return swap(block, 4)


def swap_pair(block):
    return swap(block, 2)


def swap_core(block):
    return swap(block, 1)


def add(left, right):
    return (left.astype(jnp.float32) + right.astype(jnp.float32)).astype(jnp.bfloat16)


def local(
    forward_start,
    forward_feed,
    backward_start,
    backward_feed,
    saved_inputs,
    expert_picks,
    pick_weights,
    norm_gain,
    w_gate,
    w_up,
    w_down,
):
    model_width = forward_start.shape[2]
    section_pos = lax.axis_index("section")
    section_count = lax.axis_size("section")
    expert_pos = lax.axis_index("expert")
    my_y = expert_pos // 8
    my_half = (expert_pos // 4) % 2
    gain_row = norm_gain[0].astype(jnp.float32)
    gate_w = w_gate[0]
    up_w = w_up[0]
    down_w = w_down[0]

    def normalize(token_rows):
        widened = token_rows.astype(jnp.float32)
        inverse = lax.rsqrt(jnp.mean(widened * widened, axis=-1, keepdims=True) + EPSILON)
        normed = (widened * inverse * gain_row).astype(jnp.bfloat16)
        return (widened, inverse, normed)

    def slot_table(pair_picks):
        flat_picks = pair_picks.reshape(-1)
        onehot = (flat_picks[:, None] == jnp.arange(EXPERTS, dtype=jnp.int32)[None, :]).astype(
            jnp.int32
        )
        before = jnp.cumsum(onehot, axis=0) - onehot
        rank = jnp.sum(before * onehot, axis=1)
        distance = (flat_picks // 2 - my_y + 4) % 4
        other = (flat_picks % 2) ^ my_half
        slots = (distance * 2 + other) * CAP + rank
        return (
            slots[:, None] == jnp.arange(EXPERTS * CAP, dtype=jnp.int32)[None, :]
        ).astype(jnp.bfloat16)

    def send_y(rows, placement):
        buffer = lax.dot_general(
            placement, rows, (((0,), (0,)), ((), ())), preferred_element_type=jnp.float32
        ).astype(jnp.bfloat16)
        slots = [buffer[16 * d : 16 * d + 16] for d in range(4)]
        return [slots[0]] + [y_shift(slots[d], d) for d in (1, 2, 3)]

    def split(arrived):
        kept = jnp.concatenate([a[:CAP] for a in arrived])
        crossing = jnp.concatenate([a[CAP:] for a in arrived])
        return kept, crossing

    def spread(kept, crossing):
        crossed = swap_half(crossing)
        pair = jnp.concatenate([kept, crossed, swap_pair(kept), swap_pair(crossed)])
        return pair, swap_core(pair)

    def gather_back(keep, send):
        pair = add(keep, swap_core(send))
        crossed = add(pair[32:64], swap_pair(pair[96:]))
        crossing = swap_half(crossed)
        kept = add(pair[:32], swap_pair(pair[64:96]))
        both = [
            jnp.concatenate([kept[CAP * d : CAP * d + CAP], crossing[CAP * d : CAP * d + CAP]])
            for d in range(4)
        ]
        return jnp.concatenate([both[0]] + [y_shift(both[d], -d) for d in (1, 2, 3)])

    def pick_rows(placement, sums):
        return jnp.dot(placement, sums, preferred_element_type=jnp.float32)

    def forward_send(rows, tick):
        widened, _, normed = normalize(rows)
        placement = slot_table(expert_picks[0, tick, 0])
        return widened, placement, send_y(normed, placement)

    def forward_end(widened, placement, sums, tick):
        return (widened + pick_weights[0, tick, 0] * pick_rows(placement, sums)).astype(
            jnp.bfloat16
        )

    def scale(rows, tick):
        return (pick_weights[0, tick, 1] * rows.astype(jnp.float32)).astype(jnp.bfloat16)

    def backward_end(saved, rows, placement, sums):
        wide, inverse = saved
        scaled_grad = pick_rows(placement, sums) * gain_row
        cubed = inverse * inverse * inverse
        grad_input = inverse * scaled_grad - wide * cubed * jnp.mean(
            wide * scaled_grad, axis=-1, keepdims=True
        )
        return (rows.astype(jnp.float32) + grad_input).astype(jnp.bfloat16)

    rows_f0, rows_g0 = forward_start[0], backward_start[0]
    wide_f0, place_f0, y_f0 = forward_send(rows_f0, 0)
    wide_s0, inv_s0, norm_s0 = normalize(saved_inputs[0, 0])
    place_b0 = slot_table(expert_picks[0, 0, 1])
    y_s0 = send_y(norm_s0, place_b0)
    y_g0 = send_y(scale(rows_g0, 0), place_b0)
    wide_s1, inv_s1, norm_s1 = normalize(saved_inputs[0, 1])
    place_b1 = slot_table(expert_picks[0, 1, 1])

    f0 = spread(*split(y_f0))
    s0 = spread(*split(y_s0))
    g0 = spread(*split(y_g0))
    rf0 = gather_back(*expert_forward(*f0, gate_w, up_w, down_w))
    act0 = expert_gate_up(*s0, gate_w, up_w)
    rg0 = gather_back(*expert_backward(*act0, *g0, gate_w, up_w, down_w))
    out_f0 = forward_end(wide_f0, place_f0, rf0, 0)
    rel_f = from_behind(out_f0, "section", 1)
    out_g0 = backward_end((wide_s0, inv_s0), rows_g0, place_b0, rg0)
    rel_g = from_behind(out_g0, "section", -1)

    y_s1 = send_y(norm_s1, place_b1)
    s1 = spread(*split(y_s1))
    act1 = expert_gate_up(*s1, gate_w, up_w)

    rows_f1 = jnp.where(section_pos == 0, forward_feed[0], rel_f)
    rows_g1 = jnp.where(section_pos == section_count - 1, backward_feed[0], rel_g)
    wide_f1, place_f1, y_f1 = forward_send(rows_f1, 1)
    f1 = spread(*split(y_f1))
    rf1 = gather_back(*expert_forward(*f1, gate_w, up_w, down_w))
    out_f1 = forward_end(wide_f1, place_f1, rf1, 1)
    y_g1 = send_y(scale(rows_g1, 1), place_b1)
    g1 = spread(*split(y_g1))
    rg1 = gather_back(*expert_backward(*act1, *g1, gate_w, up_w, down_w))
    out_g1 = backward_end((wide_s1, inv_s1), rows_g1, place_b1, rg1)
    return (jnp.stack([out_f0, out_f1])[None], jnp.stack([out_g0, out_g1])[None])


def solution(mesh):
    in_specs = (
        P("section", "expert", None),
        P(None, "expert", None),
        P("section", "expert", None),
        P(None, "expert", None),
        P("section", None, "expert", None),
        P("section", None, None, "expert", None),
        P("section", None, None, "expert", None),
        P("section", None),
        P("section", None, "expert"),
        P("section", None, "expert"),
        P("section", "expert", None),
    )
    out_specs = (P("section", None, "expert", None), P("section", None, "expert", None))
    return jax.shard_map(local, mesh=mesh, in_specs=in_specs, out_specs=out_specs, check_vma=False)
```
